32 devices in a mesh: groups: 2 (over y), seq: 4 (over x, core), head: 4 (over z).
Axes of the slice: x: 2, y: 2, z: 4, core: 2. Of those that a mesh axis runs over, the one named last changes fastest.
Arguments:
- query_rows: bfloat16 [8192, 16, 128], P(('groups', 'seq'), 'head'), parts along dimension 0, may hold values from -16 to 16
- key_rows: bfloat16 [8192, 16, 128], P(('groups', 'seq'), 'head'), parts along dimension 0, may hold values from -10 to 10
- value_rows: bfloat16 [8192, 16, 128], P(('groups', 'seq'), 'head'), parts along dimension 0, may hold values from -6 to 6
- grad_rows: bfloat16 [8192, 16, 128], P(('groups', 'seq'), 'head'), parts along dimension 0, may hold values from -6 to 6
- clusters: int32 [16, 8192], P('head', ('groups', 'seq')), parts along dimension 1, may hold values from 0 to 3, as said below
- positions: int32 [8192], P(('groups', 'seq')), parts along dimension 0, may hold values from 0 to 4095, each once
Outputs:
- query_grad: bfloat16 [8192, 16, 128], P(('groups', 'seq'), 'head'), parts along dimension 0
- key_grad: bfloat16 [8192, 16, 128], P(('groups', 'seq'), 'head'), parts along dimension 0
- value_grad: bfloat16 [8192, 16, 128], P(('groups', 'seq'), 'head'), parts along dimension 0
- centroid_sums: float32 [16, 8, 128], P('head', ('groups', 'seq')), parts along dimension 1
The draws below stay inside these ranges and needn't reach their ends.
There are 2 independent parts, one for each index of `groups`. The reference program is written for one: setup_inputs(seed, part) draws one part's arguments, and reference() takes and returns one part's arrays. A program takes and returns all parts, laid end to end along the dimension named above; each array names one. Nothing has to cross between parts.
Inputs may be any that keep to these rules, and one draw needn't show every extreme that they name: `clusters`: for each head every cluster holds exactly 1024 rows. Of the 1024 rows of one aligned block (the rows of one device along seq), the number whose cluster lies in one group g * 1 to g + 1 - 1 is 192, 256 or 320; in each head and block exactly one group receives 256 + 64 and exactly one 256 - 64. `positions`: each position occurs once.
All inputs are finite; a program needn't handle non-finite values.
Results may differ from the reference program's by a relative error of at most 0.012.
Values may be sent and summed in bfloat16 or wider, within the bound.
A program may use at most 128 MiB of HBM per device.

```python
import jax
import jax.numpy as jnp
from jax import lax

HEADS = 16
HD = 128
CSIZE = 1024
CL_DEV = 1
TOK_DEV = 1024
TOKENS = 4096
CLUSTERS = 4
SHARE = 256


def draw_query_rows(key, part):
    key = jax.random.fold_in(key, 21)
    values_drawn = jax.random.truncated_normal(key, -6.0, 6.0, (TOKENS, HEADS, HD), jnp.float32)
    return values_drawn.astype(jnp.bfloat16)


def draw_key_rows(key, part):
    key = jax.random.fold_in(key, 31)
    values_drawn = jax.random.truncated_normal(key, -6.0, 6.0, (TOKENS, HEADS, HD), jnp.float32)
    return values_drawn.astype(jnp.bfloat16)


def draw_clusters(key, part):
    key = jax.random.fold_in(key, 11)
    sources = TOKENS // TOK_DEV
    spare_rows = SHARE // 4

    def one_head(head_key):
        key_one, key_two, key_three = jax.random.split(head_key, 3)
        shuffle = jax.random.permutation(key_one, sources).astype(jnp.int32)
        columns = jnp.arange(sources, dtype=jnp.int32)
        raised = (columns[None, :] == shuffle[:, None]).astype(jnp.int32)
        lowered = (columns[None, :] == jnp.roll(shuffle, -1)[:, None]).astype(jnp.int32)
        counts = SHARE + spare_rows * (raised - lowered)
        block_ends = jnp.cumsum(counts, axis=1)
        starts = block_ends - counts
        column_starts = jnp.cumsum(counts, axis=0) - counts
        local_order = jax.vmap(lambda sub_key: jax.random.permutation(sub_key, TOK_DEV))(jax.random.split(key_two, sources)).astype(jnp.int32)
        target = jnp.sum((local_order[:, :, None] >= block_ends[:, None, :]).astype(jnp.int32), axis=2)
        source_index = jnp.arange(sources, dtype=jnp.int32)[:, None]
        within = local_order - starts[source_index, target]
        arrival = column_starts[source_index, target] + within
        owner_shuffle = jax.vmap(lambda sub_key: jax.random.permutation(sub_key, TOK_DEV))(jax.random.split(key_three, sources)).astype(jnp.int32)
        cluster = target * CL_DEV + owner_shuffle[target, arrival] // CSIZE
        return cluster.reshape(TOKENS).astype(jnp.int32)
    return jax.vmap(one_head)(jax.random.split(key, HEADS))


def levels(key, extent, cuts, smallest, top_value):
    level, own = 1.0, jax.random.fold_in(key, 6)
    for position, blocks in cuts:
        heights = jnp.exp(jax.random.uniform(jax.random.fold_in(own, position), (blocks,), jnp.float32, smallest / len(cuts), top_value / len(cuts)))
        level = level * jnp.repeat(heights, extent[position] // blocks).reshape([-1 if axis == position else 1 for axis in range(len(extent))])
    return level


def noise(own_key, dims, spread, most, pieces=(), kind=jnp.bfloat16):
    entries = jax.random.normal(own_key, dims, jnp.float32) * spread
    if len(pieces) > 0:
        entries = levels(own_key, dims, pieces, -0.22, 0.18) * entries
    return jnp.clip(entries, min=-most, max=most).astype(kind)


def setup_inputs(seed: int = 0, part: int = 0) -> dict:
    key_list = jax.random.split(jax.random.key(seed), 7)
    part_keys = jax.random.split(jax.random.fold_in(key_list[6], part), 7)
    query_rows = draw_query_rows(jax.random.fold_in(jax.random.fold_in(key_list[6], part), 71), part)
    key_rows = draw_key_rows(jax.random.fold_in(jax.random.fold_in(key_list[6], part), 71), part)
    value_rows = noise(part_keys[2], (TOKENS, HEADS, HD), 1.0, 6.0, ((0, 4), (1, 4)))
    grad_rows = noise(part_keys[3], (TOKENS, HEADS, HD), 1.0, 6.0, ((0, 4), (1, 4)))
    clusters = draw_clusters(jax.random.fold_in(jax.random.fold_in(key_list[6], part), 71), part)
    positions = jax.random.permutation(part_keys[5], TOKENS).astype(jnp.int32)
    return {"query_rows": query_rows, "key_rows": key_rows, "value_rows": value_rows, "grad_rows": grad_rows, "clusters": clusters, "positions": positions}


epsilon = 1e-06

def attend(query_block, key_block, value_block, grad_block, place_block):
    score_scale = query_block.shape[-1] ** (-0.5)
    scores = lax.dot_general(query_block, key_block, (((1,), (1,)), ((), ())), preferred_element_type=jnp.float32) * score_scale
    allowed = place_block[None, :] <= place_block[:, None]
    scores = jnp.where(allowed, scores, -1e+30)
    highest = lax.optimization_barrier(jnp.max(scores, axis=1, keepdims=True))
    exponent_terms = jnp.exp(scores - highest)
    weights = exponent_terms / lax.optimization_barrier(jnp.sum(exponent_terms, axis=1, keepdims=True))
    weights_low = weights.astype(jnp.bfloat16)
    output = jnp.dot(weights_low, value_block, preferred_element_type=jnp.float32)
    row_delta = lax.optimization_barrier(jnp.sum(grad_block.astype(jnp.float32) * output, axis=1, keepdims=True))
    prob_grad = lax.dot_general(grad_block, value_block, (((1,), (1,)), ((), ())), preferred_element_type=jnp.float32)
    score_grad = (weights * (prob_grad - row_delta)).astype(jnp.bfloat16)
    query_grad = (jnp.dot(score_grad, key_block, preferred_element_type=jnp.float32) * score_scale).astype(jnp.bfloat16)
    key_grad = (lax.dot_general(score_grad, query_block, (((0,), (0,)), ((), ())), preferred_element_type=jnp.float32) * score_scale).astype(jnp.bfloat16)
    value_grad = lax.dot_general(weights_low, grad_block, (((0,), (0,)), ((), ())), preferred_element_type=jnp.float32).astype(jnp.bfloat16)
    return (query_grad, key_grad, value_grad)

def unit_sum(key_block):
    key_float = key_block.astype(jnp.float32)
    unit_keys = key_float * lax.rsqrt(lax.optimization_barrier(jnp.sum(key_float * key_float, axis=1, keepdims=True)) + epsilon)
    return lax.optimization_barrier(jnp.sum(unit_keys, axis=0))

def reference(query_rows, key_rows, value_rows, grad_rows, clusters, positions):

    def one_head(head_item):
        query_head, key_head, value_head, grad_head, cluster_head = head_item
        member_order = jnp.argsort(cluster_head, stable=True).astype(jnp.int32).reshape(CLUSTERS, CSIZE)

        def one_cluster(members):
            grad_parts = attend(query_head[members], key_head[members], value_head[members], grad_head[members], positions[members])
            return (grad_parts[0], grad_parts[1], grad_parts[2], unit_sum(key_head[members]))
        query_part, key_part, value_part, centroid = lax.map(one_cluster, member_order)
        flat_order = member_order.reshape(-1)
        head_width = query_head.shape[-1]
        query_full = jnp.zeros_like(query_head).at[flat_order].set(query_part.reshape(-1, head_width))
        key_full = jnp.zeros_like(key_head).at[flat_order].set(key_part.reshape(-1, head_width))
        value_full = jnp.zeros_like(value_head).at[flat_order].set(value_part.reshape(-1, head_width))
        return (query_full, key_full, value_full, centroid)
    per_head = (jnp.moveaxis(query_rows, 1, 0), jnp.moveaxis(key_rows, 1, 0), jnp.moveaxis(value_rows, 1, 0), jnp.moveaxis(grad_rows, 1, 0), clusters)
    results = lax.map(one_head, per_head)
    return (jnp.moveaxis(results[0], 0, 1), jnp.moveaxis(results[1], 0, 1), jnp.moveaxis(results[2], 0, 1), results[3])
```

```python
import functools

import jax
import jax.numpy as jnp
from jax import lax
from jax.experimental import pallas as pl
from jax.experimental.pallas import tpu as pltpu
from jax.sharding import PartitionSpec as P

CL_DEV = 1


epsilon = 1e-06


def attend(query_block, key_block, value_block, grad_block, allowed):
    score_scale = query_block.shape[-1] ** (-0.5)
    scores = (
        lax.dot_general(
            query_block, key_block, (((1,), (1,)), ((), ())), preferred_element_type=jnp.float32
        )
        * score_scale
    )
    scores = jnp.where(allowed, scores, -1e30)
    highest = jnp.max(scores, axis=1, keepdims=True)
    exponent_terms = jnp.exp(scores - highest)
    weights = exponent_terms / jnp.sum(exponent_terms, axis=1, keepdims=True)
    weights_low = weights.astype(jnp.bfloat16)
    output = jnp.dot(weights_low, value_block, preferred_element_type=jnp.float32)
    row_delta = jnp.sum(grad_block.astype(jnp.float32) * output, axis=1, keepdims=True)
    prob_grad = lax.dot_general(
        grad_block, value_block, (((1,), (1,)), ((), ())), preferred_element_type=jnp.float32
    )
    score_grad = (weights * (prob_grad - row_delta)).astype(jnp.bfloat16)
    query_grad = (
        jnp.dot(score_grad, key_block, preferred_element_type=jnp.float32) * score_scale
    ).astype(jnp.bfloat16)
    key_grad = (
        lax.dot_general(
            score_grad, query_block, (((0,), (0,)), ((), ())), preferred_element_type=jnp.float32
        )
        * score_scale
    ).astype(jnp.bfloat16)
    value_grad = lax.dot_general(
        weights_low, grad_block, (((0,), (0,)), ((), ())), preferred_element_type=jnp.float32
    ).astype(jnp.bfloat16)
    return (query_grad, key_grad, value_grad)


def owner_head(rows_in, places_in, tags_in):
    head_width = rows_in.shape[1] // 4
    filled = tags_in > 0
    allowed = (
        (places_in[None, :] <= places_in[:, None])
        & (tags_in[None, :] == tags_in[:, None])
        & filled[None, :]
    )
    key_block = rows_in[:, head_width : 2 * head_width]
    grad_parts = attend(
        rows_in[:, :head_width],
        key_block,
        rows_in[:, 2 * head_width : 3 * head_width],
        rows_in[:, 3 * head_width :],
        allowed,
    )
    joined = jnp.concatenate(grad_parts, axis=1)
    centroid_rows = None
    key_float = key_block.astype(jnp.float32)
    unit_keys = key_float * lax.rsqrt(
        jnp.sum(key_float * key_float, axis=1, keepdims=True) + epsilon
    )
    tag_hits = (tags_in[:, None] == jnp.arange(1, CL_DEV + 1, dtype=jnp.int32)[None, :]).astype(
        jnp.float32
    )
    centroid_rows = lax.dot_general(
        tag_hits,
        unit_keys,
        (((0,), (0,)), ((), ())),
        precision=lax.Precision.HIGHEST,
        preferred_element_type=jnp.float32,
    )
    return (joined, centroid_rows)


def per_device(query_rows, key_rows, value_rows, grad_rows, clusters, positions):
    tok_count = query_rows.shape[0]
    head_width = query_rows.shape[2]
    sources = lax.axis_size("seq")
    peer_share = tok_count // sources
    capacity = peer_share + peer_share // 4
    total_slots = sources * capacity
    owner_of = clusters // CL_DEV
    local_tag = clusters % CL_DEV + 1
    owner_hits = (
        owner_of[:, :, None] == jnp.arange(sources, dtype=jnp.int32)[None, None, :]
    ).astype(jnp.int32)
    arrival = jnp.sum(jnp.cumsum(owner_hits, axis=1) * owner_hits, axis=2) - 1
    send_slot = owner_of * capacity + arrival
    slot_hits = send_slot[:, None, :] == jnp.arange(total_slots, dtype=jnp.int32)[None, :, None]
    slot_table = slot_hits.astype(jnp.bfloat16)
    payload = jnp.concatenate([query_rows, key_rows, value_rows, grad_rows], axis=2)
    send_rows = jnp.einsum(
        "hst,thd->hsd", slot_table, payload, preferred_element_type=jnp.float32
    ).astype(jnp.bfloat16)
    send_place = jnp.sum(jnp.where(slot_hits, positions[None, None, :], 0), axis=2)
    send_tag = jnp.sum(jnp.where(slot_hits, local_tag[:, None, :], 0), axis=2)
    centroid_parts = None
    rows_in = lax.all_to_all(send_rows, "seq", split_axis=1, concat_axis=1, tiled=True)
    places_in = lax.all_to_all(send_place, "seq", split_axis=1, concat_axis=1, tiled=True)
    tags_in = lax.all_to_all(send_tag, "seq", split_axis=1, concat_axis=1, tiled=True)
    grad_list = []
    centroid_list = []
    for head_at in range(rows_in.shape[0]):
        slot_grads, centroid_rows = owner_head(
            rows_in[head_at], places_in[head_at], tags_in[head_at]
        )
        grad_list.append(slot_grads)
        centroid_list.append(centroid_rows)
    stacked_grads = jnp.stack(grad_list, axis=0)
    stacked_grads, centroid_parts = (stacked_grads, jnp.stack(centroid_list, axis=0))
    returned = lax.all_to_all(stacked_grads, "seq", split_axis=1, concat_axis=1, tiled=True)
    home_rows = jnp.einsum(
        "hst,hsd->thd", slot_table, returned, preferred_element_type=jnp.float32
    ).astype(jnp.bfloat16)
    query_grad = home_rows[:, :, :head_width]
    key_grad = home_rows[:, :, head_width : 2 * head_width]
    value_grad = home_rows[:, :, 2 * head_width :]
    return (query_grad, key_grad, value_grad, centroid_parts)


def span_of(source, sources, total, low, high):
    first = max(source * low, total - (sources - source) * high)
    last = min((source + 1) * high, total - (sources - 1 - source) * low)
    return first, last


def exchange_kernel(
    sources,
    spans,
    meta_hbm,
    query_hbm,
    key_hbm,
    grad_hbm,
    value_hbm,
    dquery_hbm,
    dkey_hbm,
    dvalue_hbm,
    centroid_hbm,
    meta_in,
    pair_in,
    grad_in,
    value_in,
    pair_rows,
    grad_rows,
    value_rows,
    place_col,
    place_row,
    key_lines,
    key_cols,
    weights,
    home_pair,
    home_value,
    dvalue_rows,
    dpair_rows,
    stacked,
    centroid_out,
    send_sem,
    recv_sem,
    local_sem,
    *tables,
):
    pick = tables[:sources]
    unpick = tables[sources:]
    tokens = pair_in.shape[1]
    width = grad_in.shape[2]
    clusters = pair_rows.shape[0]
    rows = pair_rows.shape[1]
    scale = width ** (-0.5)
    me = lax.axis_index("seq")
    order = [sources // 2] + [d for d in range(1, sources) if d != sources // 2]

    def peer(d):
        return lax.rem(me + d, sources)

    def remote(array, d, src, dst):
        return pltpu.make_async_remote_copy(
            src_ref=src,
            dst_ref=dst,
            send_sem=send_sem.at[array, d - 1],
            recv_sem=recv_sem.at[array, d - 1],
            device_id={"seq": peer(d)},
            device_id_type=pl.DeviceIdType.MESH,
        )

    def exchange(array, src_at, dst):
        copies = [remote(array, d, src_at(peer(d)), dst) for d in order]
        own = pltpu.make_async_copy(src_at(me), dst, local_sem.at[array])
        for copy in copies:
            copy.start()
        own.start()
        return copies, own

    def arrive(started):
        copies, own = started
        own.wait()
        for copy in copies:
            copy.wait_recv()

    barrier = pltpu.get_barrier_semaphore()
    for d in range(1, sources):
        pl.semaphore_signal(
            barrier, inc=1, device_id={"seq": peer(d)}, device_id_type=pl.DeviceIdType.MESH
        )
    pl.semaphore_wait(barrier, sources - 1)

    meta_go = exchange(0, lambda to: meta_hbm.at[to], meta_in.at[me])
    query_go = exchange(1, lambda to: query_hbm.at[to], pair_in.at[me, :, :width])
    key_go = exchange(2, lambda to: key_hbm.at[to], pair_in.at[me, :, width:])

    tri_rows = tokens // 8

    @pl.loop(0, 8)
    def _(step):
        base = pl.multiple_of(step * tri_rows, tri_rows)
        before = lax.broadcasted_iota(jnp.int32, (tri_rows, tokens), 0) + base
        after = lax.broadcasted_iota(jnp.int32, (tri_rows, tokens), 1)
        weights[0, pl.ds(base, tri_rows), :] = jnp.where(before < after, 1.0, 0.0).astype(
            jnp.bfloat16
        )

    arrive(meta_go)
    line = lax.broadcasted_iota(jnp.int32, (8, tokens), 0)
    line_float = line.astype(jnp.float32)
    base_count = jnp.zeros((8, 1), jnp.float32)
    lines = jnp.zeros((8, tokens), jnp.float32)
    for b in range(sources):
        first, last = spans[b]
        cluster = meta_in[b, 0:1, :]
        hits = jnp.where(cluster == line_float, 1.0, 0.0)
        rank = jnp.dot(
            hits.astype(jnp.bfloat16), weights[0], preferred_element_type=jnp.float32
        )
        target = jnp.sum(hits * (rank + base_count), axis=0, keepdims=True)
        base_count = base_count + jnp.sum(hits, axis=1, keepdims=True)
        slot = cluster * float(last - first) + target - float(first)
        lines = jnp.where(line == b, slot, lines)
    key_lines[...] = lines
    key_cols[...] = jnp.transpose(lines)

    for b in range(sources):
        first, last = spans[b]
        many = clusters * (last - first)

        @pl.loop(0, many // 64)
        def _(step, b=b):
            base = pl.multiple_of(step * 64, 64)
            at = (lax.broadcasted_iota(jnp.int32, (64, tokens), 0) + base).astype(jnp.float32)
            pick[b][pl.ds(base, 64), :] = jnp.where(
                at == key_lines[b : b + 1, :], 1.0, 0.0
            ).astype(jnp.bfloat16)

        @pl.loop(0, tokens // 64)
        def _(step, b=b, many=many):
            base = pl.multiple_of(step * 64, 64)
            at = lax.broadcasted_iota(jnp.int32, (64, many), 1).astype(jnp.float32)
            unpick[b][pl.ds(base, 64), :] = jnp.where(
                at == key_cols[pl.ds(base, 64), b : b + 1], 1.0, 0.0
            ).astype(jnp.bfloat16)

    def gather(block_at, out):
        for b in range(sources):
            first, last = spans[b]
            size = last - first
            shared = spans[b - 1][1] - first if b > 0 else 0
            block = block_at(b)

            @pl.loop(0, clusters)
            def _(c, b=b, first=first, last=last, size=size, shared=shared, block=block):
                found = jnp.dot(
                    pick[b][pl.ds(pl.multiple_of(c * size, 64), size), :],
                    block,
                    preferred_element_type=jnp.float32,
                )
                if shared > 0:
                    out[c, first : first + shared, :] = (
                        out[c, first : first + shared, :].astype(jnp.float32) + found[:shared]
                    ).astype(out.dtype)
                out[c, first + shared : last, :] = found[shared:].astype(out.dtype)

    gather(lambda b: jnp.transpose(meta_in[b]).astype(jnp.bfloat16), place_col)

    @pl.loop(0, clusters)
    def _(c):
        place_row[c] = jnp.transpose(place_col[c])

    arrive(query_go)
    grad_go = exchange(3, lambda to: grad_hbm.at[to], grad_in.at[me])
    arrive(key_go)
    value_go = exchange(4, lambda to: value_hbm.at[to], value_in.at[me])
    gather(lambda b: pair_in[b], pair_rows)

    @pl.loop(0, clusters)
    def _(c):
        keys = pair_rows[c, :, width:].astype(jnp.float32)
        unit = keys * lax.rsqrt(jnp.sum(keys * keys, axis=1, keepdims=True) + epsilon)
        centroid_out[c] = jnp.broadcast_to(jnp.sum(unit, axis=0, keepdims=True), (8, width))

    centroid_go = exchange(5, lambda to: centroid_out.at[to], centroid_hbm.at[me])

    tile = min(256, rows)
    tiles = rows // tile

    @pl.loop(0, clusters * tiles)
    def _(step):
        c = step // tiles
        base = pl.multiple_of((step % tiles) * tile, tile)
        scores = lax.dot_general(
            pair_rows[c, :, width:],
            pair_rows[c, pl.ds(base, tile), :width],
            (((1,), (1,)), ((), ())),
            preferred_element_type=jnp.float32,
        )
        place_u = place_col[c, :, 1:2] * 64.0 + place_col[c, :, 2:3]
        place_t = (
            place_row[c, 1:2, pl.ds(base, tile)] * 64.0 + place_row[c, 2:3, pl.ds(base, tile)]
        )
        scores = jnp.where(place_u <= place_t, scores, -1e30)
        highest = jnp.max(scores, axis=0, keepdims=True)
        terms = jnp.exp2((scores - highest) * (scale * 1.4426950408889634))
        inverse = 1.0 / jnp.sum(terms, axis=0, keepdims=True)
        weights[c, :, pl.ds(base, tile)] = (terms * inverse).astype(jnp.bfloat16)

    def go_home(source, home, arrays):
        started = []
        wide = source.shape[2]
        turn = 256
        for d in order + [0]:
            to = peer(d)
            for b in range(sources):

                @pl.when(to == b)
                def _(b=b):
                    first, last = spans[b]
                    size = last - first
                    for c in range(clusters):
                        stacked[c * size : (c + 1) * size, :wide] = source[c, first:last, :]

                    @pl.loop(0, tokens // turn)
                    def _(step):
                        base = pl.multiple_of(step * turn, turn)
                        home[b, pl.ds(base, turn), :] = jnp.dot(
                            unpick[b][pl.ds(base, turn), :],
                            stacked[: clusters * size, :wide],
                            preferred_element_type=jnp.float32,
                        ).astype(jnp.bfloat16)

            for at, (array, target) in enumerate(arrays):
                src = home.at[to, :, at * width : (at + 1) * width]
                if d == 0:
                    copy = pltpu.make_async_copy(src, target.at[me], local_sem.at[array])
                else:
                    copy = remote(array, d, src, target.at[me])
                copy.start()
                started.append((d, copy))
        return started

    arrive(grad_go)
    gather(lambda b: grad_in[b], grad_rows)

    @pl.loop(0, clusters)
    def _(c):
        dvalue_rows[c] = jnp.dot(
            weights[c], grad_rows[c], preferred_element_type=jnp.float32
        ).astype(jnp.bfloat16)

    home_go = go_home(dvalue_rows, home_value, [(6, dvalue_hbm)])

    arrive(value_go)
    gather(lambda b: value_in[b], value_rows)

    @pl.loop(0, clusters)
    def _(c):
        keys_turned = jnp.transpose(pair_rows[c, :, width:])

        @pl.loop(0, tiles)
        def _(step):
            base = pl.multiple_of(step * tile, tile)
            prob = lax.dot_general(
                value_rows[c],
                grad_rows[c, pl.ds(base, tile), :],
                (((1,), (1,)), ((), ())),
                preferred_element_type=jnp.float32,
            )
            part = weights[c, :, pl.ds(base, tile)].astype(jnp.float32)
            delta = jnp.sum(part * prob, axis=0, keepdims=True)
            score_grad = (part * (prob - delta)).astype(jnp.bfloat16)
            weights[c, :, pl.ds(base, tile)] = score_grad
            turned = jnp.dot(keys_turned, score_grad, preferred_element_type=jnp.float32)
            dpair_rows[c, pl.ds(base, tile), :width] = jnp.transpose(turned * scale).astype(
                jnp.bfloat16
            )

        dpair_rows[c, :, width:] = (
            jnp.dot(weights[c], pair_rows[c, :, :width], preferred_element_type=jnp.float32)
            * scale
        ).astype(jnp.bfloat16)

    home_go = home_go + go_home(dpair_rows, home_pair, [(7, dquery_hbm), (8, dkey_hbm)])

    arrive(centroid_go)
    for copies, _own in (meta_go, query_go, key_go, grad_go, value_go, centroid_go):
        for copy in copies:
            copy.wait_send()
    for d, copy in home_go:
        copy.wait()


def per_device_heads(query_rows, key_rows, value_rows, grad_rows, clusters, positions):
    tokens, heads, width = query_rows.shape
    sources = lax.axis_size("seq")
    total = tokens
    share = tokens // sources
    spans = [
        span_of(b, sources, total, share - share // 4, share + share // 4) for b in range(sources)
    ]
    places = jnp.broadcast_to(positions[None, :], (heads, tokens))
    blank = jnp.zeros_like(places)
    meta = jnp.stack(
        [clusters, places // 64, places % 64, blank, blank, blank, blank, blank], axis=1
    ).astype(jnp.float32)
    by_head = [
        jnp.transpose(rows, (1, 0, 2)) for rows in (query_rows, key_rows, grad_rows, value_rows)
    ]
    anywhere = pl.BlockSpec(memory_space=pl.ANY)
    rows_shape = jax.ShapeDtypeStruct((heads, tokens, width), jnp.bfloat16)
    low = jnp.bfloat16
    full = jnp.float32
    sizes = [sources * (last - first) for first, last in spans]
    scratch = [
        pltpu.VMEM((sources, 8, tokens), full),
        pltpu.VMEM((sources, tokens, 2 * width), low),
        pltpu.VMEM((sources, tokens, width), low),
        pltpu.VMEM((sources, tokens, width), low),
        pltpu.VMEM((sources, total, 2 * width), low),
        pltpu.VMEM((sources, total, width), low),
        pltpu.VMEM((sources, total, width), low),
        pltpu.VMEM((sources, total, 8), full),
        pltpu.VMEM((sources, 8, total), full),
        pltpu.VMEM((8, tokens), full),
        pltpu.VMEM((tokens, 8), full),
        pltpu.VMEM((sources, total, total), low),
        pltpu.VMEM((sources, tokens, 2 * width), low),
        pltpu.VMEM((sources, tokens, width), low),
        pltpu.VMEM((sources, total, width), low),
        pltpu.VMEM((sources, total, 2 * width), low),
        pltpu.VMEM((max(sizes), 2 * width), low),
        pltpu.VMEM((sources, 8, width), full),
        pltpu.SemaphoreType.DMA((9, sources - 1)),
        pltpu.SemaphoreType.DMA((9, sources - 1)),
        pltpu.SemaphoreType.DMA((9,)),
    ]
    scratch += [pltpu.VMEM((size, tokens), low) for size in sizes]
    scratch += [pltpu.VMEM((tokens, size), low) for size in sizes]
    outs = pl.pallas_call(
        functools.partial(exchange_kernel, sources, spans),
        out_shape=(
            rows_shape,
            rows_shape,
            rows_shape,
            jax.ShapeDtypeStruct((heads, 8, width), full),
        ),
        in_specs=[anywhere] * 5,
        out_specs=(anywhere,) * 4,
        scratch_shapes=scratch,
        compiler_params=pltpu.CompilerParams(
            collective_id=0, has_side_effects=True, vmem_limit_bytes=62 * 1024 * 1024
        ),
    )(meta, *by_head)
    dquery, dkey, dvalue = [jnp.transpose(rows, (1, 0, 2)) for rows in outs[:3]]
    return dquery, dkey, dvalue, outs[3][:, 0:1, :]


def solution(mesh):
    sources = mesh.shape["seq"]

    def body(query_rows, *others):
        if query_rows.shape[1] == sources and CL_DEV == 1:
            return per_device_heads(query_rows, *others)
        return per_device(query_rows, *others)

    return jax.shard_map(
        body,
        mesh=mesh,
        in_specs=(
            P(("groups", "seq"), "head", None),
            P(("groups", "seq"), "head", None),
            P(("groups", "seq"), "head", None),
            P(("groups", "seq"), "head", None),
            P("head", ("groups", "seq")),
            P(("groups", "seq")),
        ),
        out_specs=(
            P(("groups", "seq"), "head", None),
            P(("groups", "seq"), "head", None),
            P(("groups", "seq"), "head", None),
            P("head", ("groups", "seq"), None),
        ),
        check_vma=False,
    )
```

```python
import functools

import jax
import jax.numpy as jnp
from jax import lax
from jax.experimental import pallas as pl
from jax.experimental.pallas import tpu as pltpu
from jax.sharding import PartitionSpec as P

CL_DEV = 1


epsilon = 1e-06


def attend(query_block, key_block, value_block, grad_block, allowed):
    score_scale = query_block.shape[-1] ** (-0.5)
    scores = (
        lax.dot_general(
            query_block, key_block, (((1,), (1,)), ((), ())), preferred_element_type=jnp.float32
        )
        * score_scale
    )
    scores = jnp.where(allowed, scores, -1e30)
    highest = jnp.max(scores, axis=1, keepdims=True)
    exponent_terms = jnp.exp(scores - highest)
    weights = exponent_terms / jnp.sum(exponent_terms, axis=1, keepdims=True)
    weights_low = weights.astype(jnp.bfloat16)
    output = jnp.dot(weights_low, value_block, preferred_element_type=jnp.float32)
    row_delta = jnp.sum(grad_block.astype(jnp.float32) * output, axis=1, keepdims=True)
    prob_grad = lax.dot_general(
        grad_block, value_block, (((1,), (1,)), ((), ())), preferred_element_type=jnp.float32
    )
    score_grad = (weights * (prob_grad - row_delta)).astype(jnp.bfloat16)
    query_grad = (
        jnp.dot(score_grad, key_block, preferred_element_type=jnp.float32) * score_scale
    ).astype(jnp.bfloat16)
    key_grad = (
        lax.dot_general(
            score_grad, query_block, (((0,), (0,)), ((), ())), preferred_element_type=jnp.float32
        )
        * score_scale
    ).astype(jnp.bfloat16)
    value_grad = lax.dot_general(
        weights_low, grad_block, (((0,), (0,)), ((), ())), preferred_element_type=jnp.float32
    ).astype(jnp.bfloat16)
    return (query_grad, key_grad, value_grad)


def owner_head(rows_in, places_in, tags_in):
    head_width = rows_in.shape[1] // 4
    filled = tags_in > 0
    allowed = (
        (places_in[None, :] <= places_in[:, None])
        & (tags_in[None, :] == tags_in[:, None])
        & filled[None, :]
    )
    key_block = rows_in[:, head_width : 2 * head_width]
    grad_parts = attend(
        rows_in[:, :head_width],
        key_block,
        rows_in[:, 2 * head_width : 3 * head_width],
        rows_in[:, 3 * head_width :],
        allowed,
    )
    joined = jnp.concatenate(grad_parts, axis=1)
    centroid_rows = None
    key_float = key_block.astype(jnp.float32)
    unit_keys = key_float * lax.rsqrt(
        jnp.sum(key_float * key_float, axis=1, keepdims=True) + epsilon
    )
    tag_hits = (tags_in[:, None] == jnp.arange(1, CL_DEV + 1, dtype=jnp.int32)[None, :]).astype(
        jnp.float32
    )
    centroid_rows = lax.dot_general(
        tag_hits,
        unit_keys,
        (((0,), (0,)), ((), ())),
        precision=lax.Precision.HIGHEST,
        preferred_element_type=jnp.float32,
    )
    return (joined, centroid_rows)


def per_device(query_rows, key_rows, value_rows, grad_rows, clusters, positions):
    tok_count = query_rows.shape[0]
    head_width = query_rows.shape[2]
    sources = lax.axis_size("seq")
    peer_share = tok_count // sources
    capacity = peer_share + peer_share // 4
    total_slots = sources * capacity
    owner_of = clusters // CL_DEV
    local_tag = clusters % CL_DEV + 1
    owner_hits = (
        owner_of[:, :, None] == jnp.arange(sources, dtype=jnp.int32)[None, None, :]
    ).astype(jnp.int32)
    arrival = jnp.sum(jnp.cumsum(owner_hits, axis=1) * owner_hits, axis=2) - 1
    send_slot = owner_of * capacity + arrival
    slot_hits = send_slot[:, None, :] == jnp.arange(total_slots, dtype=jnp.int32)[None, :, None]
    slot_table = slot_hits.astype(jnp.bfloat16)
    payload = jnp.concatenate([query_rows, key_rows, value_rows, grad_rows], axis=2)
    send_rows = jnp.einsum(
        "hst,thd->hsd", slot_table, payload, preferred_element_type=jnp.float32
    ).astype(jnp.bfloat16)
    send_place = jnp.sum(jnp.where(slot_hits, positions[None, None, :], 0), axis=2)
    send_tag = jnp.sum(jnp.where(slot_hits, local_tag[:, None, :], 0), axis=2)
    centroid_parts = None
    rows_in = lax.all_to_all(send_rows, "seq", split_axis=1, concat_axis=1, tiled=True)
    places_in = lax.all_to_all(send_place, "seq", split_axis=1, concat_axis=1, tiled=True)
    tags_in = lax.all_to_all(send_tag, "seq", split_axis=1, concat_axis=1, tiled=True)
    grad_list = []
    centroid_list = []
    for head_at in range(rows_in.shape[0]):
        slot_grads, centroid_rows = owner_head(
            rows_in[head_at], places_in[head_at], tags_in[head_at]
        )
        grad_list.append(slot_grads)
        centroid_list.append(centroid_rows)
    stacked_grads = jnp.stack(grad_list, axis=0)
    stacked_grads, centroid_parts = (stacked_grads, jnp.stack(centroid_list, axis=0))
    returned = lax.all_to_all(stacked_grads, "seq", split_axis=1, concat_axis=1, tiled=True)
    home_rows = jnp.einsum(
        "hst,hsd->thd", slot_table, returned, preferred_element_type=jnp.float32
    ).astype(jnp.bfloat16)
    query_grad = home_rows[:, :, :head_width]
    key_grad = home_rows[:, :, head_width : 2 * head_width]
    value_grad = home_rows[:, :, 2 * head_width :]
    return (query_grad, key_grad, value_grad, centroid_parts)


def span_of(source, sources, total, low, high):
    first = max(source * low, total - (sources - source) * high)
    last = min((source + 1) * high, total - (sources - 1 - source) * low)
    return first, last


def exchange_kernel(
    sources,
    spans,
    meta_hbm,
    query_hbm,
    key_hbm,
    grad_hbm,
    value_hbm,
    dquery_hbm,
    dkey_hbm,
    dvalue_hbm,
    centroid_hbm,
    meta_in,
    pair_in,
    grad_in,
    value_in,
    pair_rows,
    grad_rows,
    value_rows,
    place_col,
    place_row,
    key_lines,
    key_cols,
    weights,
    score_low,
    dvalue_rows,
    dquery_rows,
    dkey_rows,
    stacked,
    centroid_out,
    send_sem,
    recv_sem,
    local_sem,
    *tables,
):
    pick = tables[:sources]
    unpick = tables[sources:]
    tokens = pair_in.shape[1]
    width = grad_in.shape[2]
    clusters = pair_rows.shape[0]
    rows = pair_rows.shape[1]
    scale = width ** (-0.5)
    me = lax.axis_index("seq")
    order = [sources // 2] + [d for d in range(1, sources) if d != sources // 2]

    def peer(d):
        return lax.rem(me + d, sources)

    def remote(array, d, src, dst):
        return pltpu.make_async_remote_copy(
            src_ref=src,
            dst_ref=dst,
            send_sem=send_sem.at[array, d - 1],
            recv_sem=recv_sem.at[array, d - 1],
            device_id={"seq": peer(d)},
            device_id_type=pl.DeviceIdType.MESH,
        )

    def exchange(array, src_at, dst):
        copies = [remote(array, d, src_at(peer(d)), dst) for d in order]
        own = pltpu.make_async_copy(src_at(me), dst, local_sem.at[array])
        for copy in copies:
            copy.start()
        own.start()
        return copies, own

    def arrive(started):
        copies, own = started
        own.wait()
        for copy in copies:
            copy.wait_recv()

    barrier = pltpu.get_barrier_semaphore()
    for d in range(1, sources):
        pl.semaphore_signal(
            barrier, inc=1, device_id={"seq": peer(d)}, device_id_type=pl.DeviceIdType.MESH
        )
    pl.semaphore_wait(barrier, sources - 1)

    meta_go = exchange(0, lambda to: meta_hbm.at[to], meta_in.at[me])
    key_go = exchange(2, lambda to: key_hbm.at[to], pair_in.at[me, :, width:])
    query_go = exchange(1, lambda to: query_hbm.at[to], pair_in.at[me, :, :width])

    tri_rows = tokens // 8

    @pl.loop(0, 8)
    def _(step):
        base = pl.multiple_of(step * tri_rows, tri_rows)
        before = lax.broadcasted_iota(jnp.int32, (tri_rows, tokens), 0) + base
        after = lax.broadcasted_iota(jnp.int32, (tri_rows, tokens), 1)
        score_low[pl.ds(base, tri_rows), :] = jnp.where(before < after, 1.0, 0.0).astype(
            jnp.bfloat16
        )

    arrive(meta_go)
    line = lax.broadcasted_iota(jnp.int32, (8, tokens), 0)
    line_float = line.astype(jnp.float32)
    base_count = jnp.zeros((8, 1), jnp.float32)
    lines = jnp.zeros((8, tokens), jnp.float32)
    for b in range(sources):
        first, last = spans[b]
        cluster = meta_in[b, 0:1, :]
        hits = jnp.where(cluster == line_float, 1.0, 0.0)
        rank = jnp.dot(
            hits.astype(jnp.bfloat16), score_low[...], preferred_element_type=jnp.float32
        )
        target = jnp.sum(hits * (rank + base_count), axis=0, keepdims=True)
        base_count = base_count + jnp.sum(hits, axis=1, keepdims=True)
        slot = cluster * float(last - first) + target - float(first)
        lines = jnp.where(line == b, slot, lines)
    key_lines[...] = lines
    key_cols[...] = jnp.transpose(lines)

    for b in range(sources):
        first, last = spans[b]
        many = clusters * (last - first)

        @pl.loop(0, many // 64)
        def _(step, b=b):
            base = pl.multiple_of(step * 64, 64)
            at = (lax.broadcasted_iota(jnp.int32, (64, tokens), 0) + base).astype(jnp.float32)
            pick[b][pl.ds(base, 64), :] = jnp.where(
                at == key_lines[b : b + 1, :], 1.0, 0.0
            ).astype(jnp.bfloat16)

        @pl.loop(0, tokens // 64)
        def _(step, b=b, many=many):
            base = pl.multiple_of(step * 64, 64)
            at = lax.broadcasted_iota(jnp.int32, (64, many), 1).astype(jnp.float32)
            unpick[b][pl.ds(base, 64), :] = jnp.where(
                at == key_cols[pl.ds(base, 64), b : b + 1], 1.0, 0.0
            ).astype(jnp.bfloat16)

    def gather(block_at, out, lanes=slice(None)):
        for b in range(sources):
            first, last = spans[b]
            size = last - first
            shared = spans[b - 1][1] - first if b > 0 else 0
            block = block_at(b)

            found = jnp.dot(pick[b][...], block, preferred_element_type=jnp.float32)
            for c in range(clusters):
                part = found[c * size : (c + 1) * size]
                if shared > 0:
                    out[c, first : first + shared, lanes] = (
                        out[c, first : first + shared, lanes].astype(jnp.float32) + part[:shared]
                    ).astype(out.dtype)
                out[c, first + shared : last, lanes] = part[shared:].astype(out.dtype)

    gather(lambda b: jnp.transpose(meta_in[b]).astype(jnp.bfloat16), place_col)

    @pl.loop(0, clusters)
    def _(c):
        place_row[c] = jnp.transpose(place_col[c])

    arrive(key_go)
    grad_go = exchange(3, lambda to: grad_hbm.at[to], grad_in.at[me])
    gather(lambda b: pair_in[b, :, width:], pair_rows, slice(width, 2 * width))

    @pl.loop(0, clusters)
    def _(c):
        keys = pair_rows[c, :, width:].astype(jnp.float32)
        unit = keys * lax.rsqrt(jnp.sum(keys * keys, axis=1, keepdims=True) + epsilon)
        centroid_out[c] = jnp.broadcast_to(jnp.sum(unit, axis=0, keepdims=True), (8, width))

    centroid_go = exchange(5, lambda to: centroid_out.at[to], centroid_hbm.at[me])

    arrive(query_go)
    value_go = exchange(4, lambda to: value_hbm.at[to], value_in.at[me])
    gather(lambda b: pair_in[b, :, :width], pair_rows, slice(0, width))

    tile = min(256, rows)
    tiles = rows // tile

    @pl.loop(0, clusters * tiles)
    def _(step):
        c = step // tiles
        base = pl.multiple_of((step % tiles) * tile, tile)
        scores = lax.dot_general(
            pair_rows[c, :, width:],
            pair_rows[c, pl.ds(base, tile), :width],
            (((1,), (1,)), ((), ())),
            preferred_element_type=jnp.float32,
        )
        place_u = place_col[c, :, 1:2] * 64.0 + place_col[c, :, 2:3]
        place_t = (
            place_row[c, 1:2, pl.ds(base, tile)] * 64.0 + place_row[c, 2:3, pl.ds(base, tile)]
        )
        scores = jnp.where(place_u <= place_t, scores, -1e30)
        highest = jnp.max(scores, axis=0, keepdims=True)
        terms = jnp.exp2((scores - highest) * (scale * 1.4426950408889634))
        inverse = 1.0 / jnp.sum(terms, axis=0, keepdims=True)
        weights[c, :, pl.ds(base, tile)] = terms * inverse

    def go_home(source, home, lanes, array, target):
        started = []
        for d in order + [0]:
            to = peer(d)
            for b in range(sources):

                @pl.when(to == b)
                def _(b=b):
                    first, last = spans[b]
                    size = last - first
                    for c in range(clusters):
                        stacked[c * size : (c + 1) * size, :] = source[c, first:last, :]
                    home[b, :, lanes] = jnp.dot(
                        unpick[b][...],
                        stacked[: clusters * size, :],
                        preferred_element_type=jnp.float32,
                    ).astype(jnp.bfloat16)

            src = home.at[to, :, lanes]
            if d == 0:
                copy = pltpu.make_async_copy(src, target.at[me], local_sem.at[array])
            else:
                copy = remote(array, d, src, target.at[me])
            copy.start()
            started.append(copy)
        return started

    arrive(grad_go)
    gather(lambda b: grad_in[b], grad_rows)

    @pl.loop(0, clusters)
    def _(c):
        dvalue_rows[c] = jnp.dot(
            weights[c].astype(jnp.bfloat16), grad_rows[c], preferred_element_type=jnp.float32
        ).astype(jnp.bfloat16)

    home_go = go_home(dvalue_rows, grad_in, slice(None), 6, dvalue_hbm)

    arrive(value_go)
    gather(lambda b: value_in[b], value_rows)

    @pl.loop(0, clusters)
    def _(c):
        keys_turned = jnp.transpose(pair_rows[c, :, width:])

        @pl.loop(0, tiles)
        def _(step):
            base = pl.multiple_of(step * tile, tile)
            prob = lax.dot_general(
                value_rows[c],
                grad_rows[c, pl.ds(base, tile), :],
                (((1,), (1,)), ((), ())),
                preferred_element_type=jnp.float32,
            )
            part = weights[c, :, pl.ds(base, tile)]
            part_low = part.astype(jnp.bfloat16).astype(jnp.float32)
            delta = jnp.sum(part_low * prob, axis=0, keepdims=True)
            score_grad = (part * (prob - delta)).astype(jnp.bfloat16)
            score_low[:, pl.ds(base, tile)] = score_grad
            turned = jnp.dot(keys_turned, score_grad, preferred_element_type=jnp.float32)
            dquery_rows[c, pl.ds(base, tile), :] = jnp.transpose(turned * scale).astype(
                jnp.bfloat16
            )

        dkey_rows[c] = (
            jnp.dot(
                score_low[...], pair_rows[c, :, :width], preferred_element_type=jnp.float32
            )
            * scale
        ).astype(jnp.bfloat16)

    home_go += go_home(dquery_rows, pair_in, slice(0, width), 7, dquery_hbm)
    home_go += go_home(dkey_rows, pair_in, slice(width, 2 * width), 8, dkey_hbm)

    arrive(centroid_go)
    for copies, _own in (meta_go, query_go, key_go, grad_go, value_go, centroid_go):
        for copy in copies:
            copy.wait_send()
    for copy in home_go:
        copy.wait()


def per_device_heads(query_rows, key_rows, value_rows, grad_rows, clusters, positions):
    tokens, heads, width = query_rows.shape
    sources = lax.axis_size("seq")
    total = tokens
    share = tokens // sources
    spans = [
        span_of(b, sources, total, share - share // 4, share + share // 4) for b in range(sources)
    ]
    places = jnp.broadcast_to(positions[None, :], (heads, tokens))
    blank = jnp.zeros_like(places)
    meta = jnp.stack(
        [clusters, places // 64, places % 64, blank, blank, blank, blank, blank], axis=1
    ).astype(jnp.float32)
    by_head = [
        jnp.transpose(rows, (1, 0, 2)) for rows in (query_rows, key_rows, grad_rows, value_rows)
    ]
    anywhere = pl.BlockSpec(memory_space=pl.ANY)
    rows_shape = jax.ShapeDtypeStruct((heads, tokens, width), jnp.bfloat16)
    low = jnp.bfloat16
    full = jnp.float32
    sizes = [sources * (last - first) for first, last in spans]
    scratch = [
        pltpu.VMEM((sources, 8, tokens), full),
        pltpu.VMEM((sources, tokens, 2 * width), low),
        pltpu.VMEM((sources, tokens, width), low),
        pltpu.VMEM((sources, tokens, width), low),
        pltpu.VMEM((sources, total, 2 * width), low),
        pltpu.VMEM((sources, total, width), low),
        pltpu.VMEM((sources, total, width), low),
        pltpu.VMEM((sources, total, 8), full),
        pltpu.VMEM((sources, 8, total), full),
        pltpu.VMEM((8, tokens), full),
        pltpu.VMEM((tokens, 8), full),
        pltpu.VMEM((sources, total, total), full),
        pltpu.VMEM((total, total), low),
        pltpu.VMEM((sources, total, width), low),
        pltpu.VMEM((sources, total, width), low),
        pltpu.VMEM((sources, total, width), low),
        pltpu.VMEM((max(sizes), width), low),
        pltpu.VMEM((sources, 8, width), full),
        pltpu.SemaphoreType.DMA((9, sources - 1)),
        pltpu.SemaphoreType.DMA((9, sources - 1)),
        pltpu.SemaphoreType.DMA((9,)),
    ]
    scratch += [pltpu.VMEM((size, tokens), low) for size in sizes]
    scratch += [pltpu.VMEM((tokens, size), low) for size in sizes]
    outs = pl.pallas_call(
        functools.partial(exchange_kernel, sources, spans),
        out_shape=(
            rows_shape,
            rows_shape,
            rows_shape,
            jax.ShapeDtypeStruct((heads, 8, width), full),
        ),
        in_specs=[anywhere] * 5,
        out_specs=(anywhere,) * 4,
        scratch_shapes=scratch,
        compiler_params=pltpu.CompilerParams(
            collective_id=0, has_side_effects=True, vmem_limit_bytes=62 * 1024 * 1024
        ),
    )(meta, *by_head)
    dquery, dkey, dvalue = [jnp.transpose(rows, (1, 0, 2)) for rows in outs[:3]]
    return dquery, dkey, dvalue, outs[3][:, 0:1, :]


def solution(mesh):
    sources = mesh.shape["seq"]

    def body(query_rows, *others):
        if query_rows.shape[1] == sources and CL_DEV == 1:
            return per_device_heads(query_rows, *others)
        return per_device(query_rows, *others)

    return jax.shard_map(
        body,
        mesh=mesh,
        in_specs=(
            P(("groups", "seq"), "head", None),
            P(("groups", "seq"), "head", None),
            P(("groups", "seq"), "head", None),
            P(("groups", "seq"), "head", None),
            P("head", ("groups", "seq")),
            P(("groups", "seq")),
        ),
        out_specs=(
            P(("groups", "seq"), "head", None),
            P(("groups", "seq"), "head", None),
            P(("groups", "seq"), "head", None),
            P("head", ("groups", "seq"), None),
        ),
        check_vma=False,
    )
```

```python
import functools

import jax
import jax.numpy as jnp
from jax import lax
from jax.experimental import pallas as pl
from jax.experimental.pallas import tpu as pltpu
from jax.sharding import PartitionSpec as P

CL_DEV = 1


epsilon = 1e-06


def attend(query_block, key_block, value_block, grad_block, allowed):
    score_scale = query_block.shape[-1] ** (-0.5)
    scores = (
        lax.dot_general(
            query_block, key_block, (((1,), (1,)), ((), ())), preferred_element_type=jnp.float32
        )
        * score_scale
    )
    scores = jnp.where(allowed, scores, -1e30)
    highest = jnp.max(scores, axis=1, keepdims=True)
    exponent_terms = jnp.exp(scores - highest)
    weights = exponent_terms / jnp.sum(exponent_terms, axis=1, keepdims=True)
    weights_low = weights.astype(jnp.bfloat16)
    output = jnp.dot(weights_low, value_block, preferred_element_type=jnp.float32)
    row_delta = jnp.sum(grad_block.astype(jnp.float32) * output, axis=1, keepdims=True)
    prob_grad = lax.dot_general(
        grad_block, value_block, (((1,), (1,)), ((), ())), preferred_element_type=jnp.float32
    )
    score_grad = (weights * (prob_grad - row_delta)).astype(jnp.bfloat16)
    query_grad = (
        jnp.dot(score_grad, key_block, preferred_element_type=jnp.float32) * score_scale
    ).astype(jnp.bfloat16)
    key_grad = (
        lax.dot_general(
            score_grad, query_block, (((0,), (0,)), ((), ())), preferred_element_type=jnp.float32
        )
        * score_scale
    ).astype(jnp.bfloat16)
    value_grad = lax.dot_general(
        weights_low, grad_block, (((0,), (0,)), ((), ())), preferred_element_type=jnp.float32
    ).astype(jnp.bfloat16)
    return (query_grad, key_grad, value_grad)


def owner_head(rows_in, places_in, tags_in):
    head_width = rows_in.shape[1] // 4
    filled = tags_in > 0
    allowed = (
        (places_in[None, :] <= places_in[:, None])
        & (tags_in[None, :] == tags_in[:, None])
        & filled[None, :]
    )
    key_block = rows_in[:, head_width : 2 * head_width]
    grad_parts = attend(
        rows_in[:, :head_width],
        key_block,
        rows_in[:, 2 * head_width : 3 * head_width],
        rows_in[:, 3 * head_width :],
        allowed,
    )
    joined = jnp.concatenate(grad_parts, axis=1)
    centroid_rows = None
    key_float = key_block.astype(jnp.float32)
    unit_keys = key_float * lax.rsqrt(
        jnp.sum(key_float * key_float, axis=1, keepdims=True) + epsilon
    )
    tag_hits = (tags_in[:, None] == jnp.arange(1, CL_DEV + 1, dtype=jnp.int32)[None, :]).astype(
        jnp.float32
    )
    centroid_rows = lax.dot_general(
        tag_hits,
        unit_keys,
        (((0,), (0,)), ((), ())),
        precision=lax.Precision.HIGHEST,
        preferred_element_type=jnp.float32,
    )
    return (joined, centroid_rows)


def per_device(query_rows, key_rows, value_rows, grad_rows, clusters, positions):
    tok_count = query_rows.shape[0]
    head_width = query_rows.shape[2]
    sources = lax.axis_size("seq")
    peer_share = tok_count // sources
    capacity = peer_share + peer_share // 4
    total_slots = sources * capacity
    owner_of = clusters // CL_DEV
    local_tag = clusters % CL_DEV + 1
    owner_hits = (
        owner_of[:, :, None] == jnp.arange(sources, dtype=jnp.int32)[None, None, :]
    ).astype(jnp.int32)
    arrival = jnp.sum(jnp.cumsum(owner_hits, axis=1) * owner_hits, axis=2) - 1
    send_slot = owner_of * capacity + arrival
    slot_hits = send_slot[:, None, :] == jnp.arange(total_slots, dtype=jnp.int32)[None, :, None]
    slot_table = slot_hits.astype(jnp.bfloat16)
    payload = jnp.concatenate([query_rows, key_rows, value_rows, grad_rows], axis=2)
    send_rows = jnp.einsum(
        "hst,thd->hsd", slot_table, payload, preferred_element_type=jnp.float32
    ).astype(jnp.bfloat16)
    send_place = jnp.sum(jnp.where(slot_hits, positions[None, None, :], 0), axis=2)
    send_tag = jnp.sum(jnp.where(slot_hits, local_tag[:, None, :], 0), axis=2)
    centroid_parts = None
    rows_in = lax.all_to_all(send_rows, "seq", split_axis=1, concat_axis=1, tiled=True)
    places_in = lax.all_to_all(send_place, "seq", split_axis=1, concat_axis=1, tiled=True)
    tags_in = lax.all_to_all(send_tag, "seq", split_axis=1, concat_axis=1, tiled=True)
    grad_list = []
    centroid_list = []
    for head_at in range(rows_in.shape[0]):
        slot_grads, centroid_rows = owner_head(
            rows_in[head_at], places_in[head_at], tags_in[head_at]
        )
        grad_list.append(slot_grads)
        centroid_list.append(centroid_rows)
    stacked_grads = jnp.stack(grad_list, axis=0)
    stacked_grads, centroid_parts = (stacked_grads, jnp.stack(centroid_list, axis=0))
    returned = lax.all_to_all(stacked_grads, "seq", split_axis=1, concat_axis=1, tiled=True)
    home_rows = jnp.einsum(
        "hst,hsd->thd", slot_table, returned, preferred_element_type=jnp.float32
    ).astype(jnp.bfloat16)
    query_grad = home_rows[:, :, :head_width]
    key_grad = home_rows[:, :, head_width : 2 * head_width]
    value_grad = home_rows[:, :, 2 * head_width :]
    return (query_grad, key_grad, value_grad, centroid_parts)


def span_of(source, sources, total, low, high):
    first = max(source * low, total - (sources - source) * high)
    last = min((source + 1) * high, total - (sources - 1 - source) * low)
    return first, last


def exchange_kernel(
    sources,
    spans,
    meta_hbm,
    query_hbm,
    key_hbm,
    grad_hbm,
    value_hbm,
    dquery_hbm,
    dkey_hbm,
    dvalue_hbm,
    centroid_hbm,
    meta_in,
    pair_in,
    grad_in,
    value_in,
    pair_rows,
    grad_rows,
    value_rows,
    place_col,
    place_row,
    key_lines,
    key_cols,
    weights,
    score_low,
    dvalue_rows,
    dquery_rows,
    dkey_rows,
    stacked,
    centroid_out,
    send_sem,
    recv_sem,
    local_sem,
    *tables,
):
    pick = tables[:sources]
    unpick = tables[sources:]
    tokens = pair_in.shape[1]
    width = grad_in.shape[2]
    clusters = pair_rows.shape[0]
    rows = pair_rows.shape[1]
    scale = width ** (-0.5)
    me = lax.axis_index("seq")
    order = [sources // 2] + [d for d in range(1, sources) if d != sources // 2]

    def peer(d):
        return lax.rem(me + d, sources)

    def remote(array, d, src, dst):
        return pltpu.make_async_remote_copy(
            src_ref=src,
            dst_ref=dst,
            send_sem=send_sem.at[array, d - 1],
            recv_sem=recv_sem.at[array, d - 1],
            device_id={"seq": peer(d)},
            device_id_type=pl.DeviceIdType.MESH,
        )

    def exchange(array, src_at, dst):
        copies = [remote(array, d, src_at(peer(d)), dst) for d in order]
        own = pltpu.make_async_copy(src_at(me), dst, local_sem.at[array])
        for copy in copies:
            copy.start()
        own.start()
        return copies, own

    def arrive(started):
        copies, own = started
        own.wait()
        for copy in copies:
            copy.wait_recv()

    barrier = pltpu.get_barrier_semaphore()
    for d in range(1, sources):
        pl.semaphore_signal(
            barrier, inc=1, device_id={"seq": peer(d)}, device_id_type=pl.DeviceIdType.MESH
        )
    pl.semaphore_wait(barrier, sources - 1)

    meta_go = exchange(0, lambda to: meta_hbm.at[to], meta_in.at[me])
    key_go = exchange(2, lambda to: key_hbm.at[to], pair_in.at[me, :, width:])
    query_go = exchange(1, lambda to: query_hbm.at[to], pair_in.at[me, :, :width])

    tri_rows = tokens // 8

    @pl.loop(0, 8)
    def _(step):
        base = pl.multiple_of(step * tri_rows, tri_rows)
        before = lax.broadcasted_iota(jnp.int32, (tri_rows, tokens), 0) + base
        after = lax.broadcasted_iota(jnp.int32, (tri_rows, tokens), 1)
        score_low[pl.ds(base, tri_rows), :] = jnp.where(before < after, 1.0, 0.0).astype(
            jnp.bfloat16
        )

    arrive(meta_go)
    line = lax.broadcasted_iota(jnp.int32, (8, tokens), 0)
    line_float = line.astype(jnp.float32)
    base_count = jnp.zeros((8, 1), jnp.float32)
    lines = jnp.zeros((8, tokens), jnp.float32)
    for b in range(sources):
        first, last = spans[b]
        cluster = meta_in[b, 0:1, :]
        hits = jnp.where(cluster == line_float, 1.0, 0.0)
        rank = jnp.dot(
            hits.astype(jnp.bfloat16), score_low[...], preferred_element_type=jnp.float32
        )
        target = jnp.sum(hits * (rank + base_count), axis=0, keepdims=True)
        base_count = base_count + jnp.sum(hits, axis=1, keepdims=True)
        slot = cluster * float(last - first) + target - float(first)
        lines = jnp.where(line == b, slot, lines)
    key_lines[...] = lines
    key_cols[...] = jnp.transpose(lines)

    for b in range(sources):
        first, last = spans[b]
        many = clusters * (last - first)

        @pl.loop(0, many // 64)
        def _(step, b=b):
            base = pl.multiple_of(step * 64, 64)
            at = (lax.broadcasted_iota(jnp.int32, (64, tokens), 0) + base).astype(jnp.float32)
            pick[b][pl.ds(base, 64), :] = jnp.where(
                at == key_lines[b : b + 1, :], 1.0, 0.0
            ).astype(jnp.bfloat16)

        @pl.loop(0, tokens // 64)
        def _(step, b=b, many=many):
            base = pl.multiple_of(step * 64, 64)
            at = lax.broadcasted_iota(jnp.int32, (64, many), 1).astype(jnp.float32)
            unpick[b][pl.ds(base, 64), :] = jnp.where(
                at == key_cols[pl.ds(base, 64), b : b + 1], 1.0, 0.0
            ).astype(jnp.bfloat16)

    def gather(block_at, out, lanes=slice(None)):
        for b in range(sources):
            first, last = spans[b]
            size = last - first
            shared = spans[b - 1][1] - first if b > 0 else 0
            block = block_at(b)

            together = 2 if clusters % 2 == 0 else 1

            @pl.loop(0, clusters // together)
            def _(step, b=b, first=first, last=last, size=size, shared=shared, block=block):
                base = pl.multiple_of(step * together * size, 64)
                found = jnp.dot(
                    pick[b][pl.ds(base, together * size), :],
                    block,
                    preferred_element_type=jnp.float32,
                )
                for at in range(together):
                    c = step * together + at
                    part = found[at * size : (at + 1) * size]
                    if shared > 0:
                        out[c, first : first + shared, lanes] = (
                            out[c, first : first + shared, lanes].astype(jnp.float32)
                            + part[:shared]
                        ).astype(out.dtype)
                    out[c, first + shared : last, lanes] = part[shared:].astype(out.dtype)

    gather(lambda b: jnp.transpose(meta_in[b]).astype(jnp.bfloat16), place_col)

    @pl.loop(0, clusters)
    def _(c):
        place_row[c] = jnp.transpose(place_col[c])

    arrive(key_go)
    grad_go = exchange(3, lambda to: grad_hbm.at[to], grad_in.at[me])
    gather(lambda b: pair_in[b, :, width:], pair_rows, slice(width, 2 * width))

    @pl.loop(0, clusters)
    def _(c):
        keys = pair_rows[c, :, width:].astype(jnp.float32)
        unit = keys * lax.rsqrt(jnp.sum(keys * keys, axis=1, keepdims=True) + epsilon)
        centroid_out[c] = jnp.broadcast_to(jnp.sum(unit, axis=0, keepdims=True), (8, width))

    centroid_go = exchange(5, lambda to: centroid_out.at[to], centroid_hbm.at[me])

    arrive(query_go)
    value_go = exchange(4, lambda to: value_hbm.at[to], value_in.at[me])
    gather(lambda b: pair_in[b, :, :width], pair_rows, slice(0, width))

    tile = min(256, rows)
    tiles = rows // tile

    @pl.loop(0, clusters * tiles)
    def _(step):
        c = step // tiles
        base = pl.multiple_of((step % tiles) * tile, tile)
        scores = lax.dot_general(
            pair_rows[c, :, width:],
            pair_rows[c, pl.ds(base, tile), :width],
            (((1,), (1,)), ((), ())),
            preferred_element_type=jnp.float32,
        )
        place_u = place_col[c, :, 1:2] * 64.0 + place_col[c, :, 2:3]
        place_t = (
            place_row[c, 1:2, pl.ds(base, tile)] * 64.0 + place_row[c, 2:3, pl.ds(base, tile)]
        )
        scores = jnp.where(place_u <= place_t, scores, -1e30)
        highest = jnp.max(scores, axis=0, keepdims=True)
        terms = jnp.exp2((scores - highest) * (scale * 1.4426950408889634))
        inverse = 1.0 / jnp.sum(terms, axis=0, keepdims=True)
        weights[c, :, pl.ds(base, tile)] = terms * inverse

    def go_home(source, home, lanes, array, target):
        half = sources // 2
        turn = tokens // 2

        @pl.loop(0, sources)
        def _(step):
            late = step // half
            d = (half + step) * (1 - late) + (sources - 1 - step) * late
            to = peer(d)
            for b in range(sources):

                @pl.when(to == b)
                def _(b=b):
                    first, last = spans[b]
                    size = last - first
                    for c in range(clusters):
                        stacked[c * size : (c + 1) * size, :] = source[c, first:last, :]

                    @pl.loop(0, tokens // turn)
                    def _(part):
                        base = pl.multiple_of(part * turn, turn)
                        home[b, pl.ds(base, turn), lanes] = jnp.dot(
                            unpick[b][pl.ds(base, turn), :],
                            stacked[: clusters * size, :],
                            preferred_element_type=jnp.float32,
                        ).astype(jnp.bfloat16)

            @pl.when(step < sources - 1)
            def _():
                remote(array, d, home.at[to, :, lanes], target.at[me]).start()

        own = pltpu.make_async_copy(home.at[me, :, lanes], target.at[me], local_sem.at[array])
        own.start()
        return [
            remote(array, d, home.at[peer(d), :, lanes], target.at[me])
            for d in range(1, sources)
        ] + [own]

    arrive(grad_go)
    gather(lambda b: grad_in[b], grad_rows)

    @pl.loop(0, clusters)
    def _(c):
        dvalue_rows[c] = jnp.dot(
            weights[c].astype(jnp.bfloat16), grad_rows[c], preferred_element_type=jnp.float32
        ).astype(jnp.bfloat16)

    home_go = go_home(dvalue_rows, grad_in, slice(None), 6, dvalue_hbm)

    arrive(value_go)
    gather(lambda b: value_in[b], value_rows)

    @pl.loop(0, clusters)
    def _(c):
        keys_turned = jnp.transpose(pair_rows[c, :, width:])

        @pl.loop(0, tiles)
        def _(step):
            base = pl.multiple_of(step * tile, tile)
            prob = lax.dot_general(
                value_rows[c],
                grad_rows[c, pl.ds(base, tile), :],
                (((1,), (1,)), ((), ())),
                preferred_element_type=jnp.float32,
            )
            part = weights[c, :, pl.ds(base, tile)]
            part_low = part.astype(jnp.bfloat16).astype(jnp.float32)
            delta = jnp.sum(part_low * prob, axis=0, keepdims=True)
            score_grad = (part * (prob - delta)).astype(jnp.bfloat16)
            score_low[:, pl.ds(base, tile)] = score_grad
            turned = jnp.dot(keys_turned, score_grad, preferred_element_type=jnp.float32)
            dquery_rows[c, pl.ds(base, tile), :] = jnp.transpose(turned * scale).astype(
                jnp.bfloat16
            )

        dkey_rows[c] = (
            jnp.dot(
                score_low[...], pair_rows[c, :, :width], preferred_element_type=jnp.float32
            )
            * scale
        ).astype(jnp.bfloat16)

    home_go += go_home(dquery_rows, pair_in, slice(0, width), 7, dquery_hbm)
    home_go += go_home(dkey_rows, pair_in, slice(width, 2 * width), 8, dkey_hbm)

    arrive(centroid_go)
    for copies, _own in (meta_go, query_go, key_go, grad_go, value_go, centroid_go):
        for copy in copies:
            copy.wait_send()
    for copy in home_go:
        copy.wait()


def per_device_heads(query_rows, key_rows, value_rows, grad_rows, clusters, positions):
    tokens, heads, width = query_rows.shape
    sources = lax.axis_size("seq")
    total = tokens
    share = tokens // sources
    spans = [
        span_of(b, sources, total, share - share // 4, share + share // 4) for b in range(sources)
    ]
    places = jnp.broadcast_to(positions[None, :], (heads, tokens))
    blank = jnp.zeros_like(places)
    meta = jnp.stack(
        [clusters, places // 64, places % 64, blank, blank, blank, blank, blank], axis=1
    ).astype(jnp.float32)
    by_head = [
        jnp.transpose(rows, (1, 0, 2)) for rows in (query_rows, key_rows, grad_rows, value_rows)
    ]
    anywhere = pl.BlockSpec(memory_space=pl.ANY)
    rows_shape = jax.ShapeDtypeStruct((heads, tokens, width), jnp.bfloat16)
    low = jnp.bfloat16
    full = jnp.float32
    sizes = [sources * (last - first) for first, last in spans]
    scratch = [
        pltpu.VMEM((sources, 8, tokens), full),
        pltpu.VMEM((sources, tokens, 2 * width), low),
        pltpu.VMEM((sources, tokens, width), low),
        pltpu.VMEM((sources, tokens, width), low),
        pltpu.VMEM((sources, total, 2 * width), low),
        pltpu.VMEM((sources, total, width), low),
        pltpu.VMEM((sources, total, width), low),
        pltpu.VMEM((sources, total, 8), full),
        pltpu.VMEM((sources, 8, total), full),
        pltpu.VMEM((8, tokens), full),
        pltpu.VMEM((tokens, 8), full),
        pltpu.VMEM((sources, total, total), full),
        pltpu.VMEM((total, total), low),
        pltpu.VMEM((sources, total, width), low),
        pltpu.VMEM((sources, total, width), low),
        pltpu.VMEM((sources, total, width), low),
        pltpu.VMEM((max(sizes), width), low),
        pltpu.VMEM((sources, 8, width), full),
        pltpu.SemaphoreType.DMA((9, sources - 1)),
        pltpu.SemaphoreType.DMA((9, sources - 1)),
        pltpu.SemaphoreType.DMA((9,)),
    ]
    scratch += [pltpu.VMEM((size, tokens), low) for size in sizes]
    scratch += [pltpu.VMEM((tokens, size), low) for size in sizes]
    outs = pl.pallas_call(
        functools.partial(exchange_kernel, sources, spans),
        out_shape=(
            rows_shape,
            rows_shape,
            rows_shape,
            jax.ShapeDtypeStruct((heads, 8, width), full),
        ),
        in_specs=[anywhere] * 5,
        out_specs=(anywhere,) * 4,
        scratch_shapes=scratch,
        compiler_params=pltpu.CompilerParams(
            collective_id=0, has_side_effects=True, vmem_limit_bytes=62 * 1024 * 1024
        ),
    )(meta, *by_head)
    dquery, dkey, dvalue = [jnp.transpose(rows, (1, 0, 2)) for rows in outs[:3]]
    return dquery, dkey, dvalue, outs[3][:, 0:1, :]


def solution(mesh):
    sources = mesh.shape["seq"]

    def body(query_rows, *others):
        if query_rows.shape[1] == sources and sources % 2 == 0 and CL_DEV == 1:
            return per_device_heads(query_rows, *others)
        return per_device(query_rows, *others)

    return jax.shard_map(
        body,
        mesh=mesh,
        in_specs=(
            P(("groups", "seq"), "head", None),
            P(("groups", "seq"), "head", None),
            P(("groups", "seq"), "head", None),
            P(("groups", "seq"), "head", None),
            P("head", ("groups", "seq")),
            P(("groups", "seq")),
        ),
        out_specs=(
            P(("groups", "seq"), "head", None),
            P(("groups", "seq"), "head", None),
            P(("groups", "seq"), "head", None),
            P("head", ("groups", "seq"), None),
        ),
        check_vma=False,
    )
```

```python
import functools

import jax
import jax.numpy as jnp
from jax import lax
from jax.experimental import pallas as pl
from jax.experimental.pallas import tpu as pltpu
from jax.sharding import PartitionSpec as P

CL_DEV = 1


epsilon = 1e-06


def attend(query_block, key_block, value_block, grad_block, allowed):
    score_scale = query_block.shape[-1] ** (-0.5)
    scores = (
        lax.dot_general(
            query_block, key_block, (((1,), (1,)), ((), ())), preferred_element_type=jnp.float32
        )
        * score_scale
    )
    scores = jnp.where(allowed, scores, -1e30)
    highest = jnp.max(scores, axis=1, keepdims=True)
    exponent_terms = jnp.exp(scores - highest)
    weights = exponent_terms / jnp.sum(exponent_terms, axis=1, keepdims=True)
    weights_low = weights.astype(jnp.bfloat16)
    output = jnp.dot(weights_low, value_block, preferred_element_type=jnp.float32)
    row_delta = jnp.sum(grad_block.astype(jnp.float32) * output, axis=1, keepdims=True)
    prob_grad = lax.dot_general(
        grad_block, value_block, (((1,), (1,)), ((), ())), preferred_element_type=jnp.float32
    )
    score_grad = (weights * (prob_grad - row_delta)).astype(jnp.bfloat16)
    query_grad = (
        jnp.dot(score_grad, key_block, preferred_element_type=jnp.float32) * score_scale
    ).astype(jnp.bfloat16)
    key_grad = (
        lax.dot_general(
            score_grad, query_block, (((0,), (0,)), ((), ())), preferred_element_type=jnp.float32
        )
        * score_scale
    ).astype(jnp.bfloat16)
    value_grad = lax.dot_general(
        weights_low, grad_block, (((0,), (0,)), ((), ())), preferred_element_type=jnp.float32
    ).astype(jnp.bfloat16)
    return (query_grad, key_grad, value_grad)


def owner_head(rows_in, places_in, tags_in):
    head_width = rows_in.shape[1] // 4
    filled = tags_in > 0
    allowed = (
        (places_in[None, :] <= places_in[:, None])
        & (tags_in[None, :] == tags_in[:, None])
        & filled[None, :]
    )
    key_block = rows_in[:, head_width : 2 * head_width]
    grad_parts = attend(
        rows_in[:, :head_width],
        key_block,
        rows_in[:, 2 * head_width : 3 * head_width],
        rows_in[:, 3 * head_width :],
        allowed,
    )
    joined = jnp.concatenate(grad_parts, axis=1)
    centroid_rows = None
    key_float = key_block.astype(jnp.float32)
    unit_keys = key_float * lax.rsqrt(
        jnp.sum(key_float * key_float, axis=1, keepdims=True) + epsilon
    )
    tag_hits = (tags_in[:, None] == jnp.arange(1, CL_DEV + 1, dtype=jnp.int32)[None, :]).astype(
        jnp.float32
    )
    centroid_rows = lax.dot_general(
        tag_hits,
        unit_keys,
        (((0,), (0,)), ((), ())),
        precision=lax.Precision.HIGHEST,
        preferred_element_type=jnp.float32,
    )
    return (joined, centroid_rows)


def per_device(query_rows, key_rows, value_rows, grad_rows, clusters, positions):
    tok_count = query_rows.shape[0]
    head_width = query_rows.shape[2]
    sources = lax.axis_size("seq")
    peer_share = tok_count // sources
    capacity = peer_share + peer_share // 4
    total_slots = sources * capacity
    owner_of = clusters // CL_DEV
    local_tag = clusters % CL_DEV + 1
    owner_hits = (
        owner_of[:, :, None] == jnp.arange(sources, dtype=jnp.int32)[None, None, :]
    ).astype(jnp.int32)
    arrival = jnp.sum(jnp.cumsum(owner_hits, axis=1) * owner_hits, axis=2) - 1
    send_slot = owner_of * capacity + arrival
    slot_hits = send_slot[:, None, :] == jnp.arange(total_slots, dtype=jnp.int32)[None, :, None]
    slot_table = slot_hits.astype(jnp.bfloat16)
    payload = jnp.concatenate([query_rows, key_rows, value_rows, grad_rows], axis=2)
    send_rows = jnp.einsum(
        "hst,thd->hsd", slot_table, payload, preferred_element_type=jnp.float32
    ).astype(jnp.bfloat16)
    send_place = jnp.sum(jnp.where(slot_hits, positions[None, None, :], 0), axis=2)
    send_tag = jnp.sum(jnp.where(slot_hits, local_tag[:, None, :], 0), axis=2)
    centroid_parts = None
    rows_in = lax.all_to_all(send_rows, "seq", split_axis=1, concat_axis=1, tiled=True)
    places_in = lax.all_to_all(send_place, "seq", split_axis=1, concat_axis=1, tiled=True)
    tags_in = lax.all_to_all(send_tag, "seq", split_axis=1, concat_axis=1, tiled=True)
    grad_list = []
    centroid_list = []
    for head_at in range(rows_in.shape[0]):
        slot_grads, centroid_rows = owner_head(
            rows_in[head_at], places_in[head_at], tags_in[head_at]
        )
        grad_list.append(slot_grads)
        centroid_list.append(centroid_rows)
    stacked_grads = jnp.stack(grad_list, axis=0)
    stacked_grads, centroid_parts = (stacked_grads, jnp.stack(centroid_list, axis=0))
    returned = lax.all_to_all(stacked_grads, "seq", split_axis=1, concat_axis=1, tiled=True)
    home_rows = jnp.einsum(
        "hst,hsd->thd", slot_table, returned, preferred_element_type=jnp.float32
    ).astype(jnp.bfloat16)
    query_grad = home_rows[:, :, :head_width]
    key_grad = home_rows[:, :, head_width : 2 * head_width]
    value_grad = home_rows[:, :, 2 * head_width :]
    return (query_grad, key_grad, value_grad, centroid_parts)


def span_of(source, sources, total, low, high):
    first = max(source * low, total - (sources - source) * high)
    last = min((source + 1) * high, total - (sources - 1 - source) * low)
    return first, last


def exchange_kernel(
    sources,
    spans,
    meta_hbm,
    query_hbm,
    key_hbm,
    grad_hbm,
    value_hbm,
    dquery_hbm,
    dkey_hbm,
    dvalue_hbm,
    centroid_hbm,
    meta_in,
    pair_in,
    grad_in,
    value_in,
    pair_rows,
    grad_rows,
    value_rows,
    place_col,
    place_row,
    key_lines,
    key_cols,
    weights,
    score_low,
    dvalue_rows,
    dquery_rows,
    dkey_rows,
    stacked,
    centroid_out,
    send_sem,
    recv_sem,
    local_sem,
    *tables,
):
    pick = tables[:sources]
    unpick = tables[sources:]
    tokens = pair_in.shape[1]
    width = grad_in.shape[2]
    clusters = pair_rows.shape[0]
    rows = pair_rows.shape[1]
    scale = width ** (-0.5)
    me = lax.axis_index("seq")
    order = [sources // 2] + [d for d in range(1, sources) if d != sources // 2]

    def peer(d):
        return lax.rem(me + d, sources)

    def remote(array, d, src, dst):
        return pltpu.make_async_remote_copy(
            src_ref=src,
            dst_ref=dst,
            send_sem=send_sem.at[array, d - 1],
            recv_sem=recv_sem.at[array, d - 1],
            device_id={"seq": peer(d)},
            device_id_type=pl.DeviceIdType.MESH,
        )

    def exchange(array, src_at, dst):
        copies = [remote(array, d, src_at(peer(d)), dst) for d in order]
        own = pltpu.make_async_copy(src_at(me), dst, local_sem.at[array])
        for copy in copies:
            copy.start()
        own.start()
        return copies, own

    def arrive(started):
        copies, own = started
        own.wait()
        for copy in copies:
            copy.wait_recv()

    barrier = pltpu.get_barrier_semaphore()
    for d in range(1, sources):
        pl.semaphore_signal(
            barrier, inc=1, device_id={"seq": peer(d)}, device_id_type=pl.DeviceIdType.MESH
        )
    pl.semaphore_wait(barrier, sources - 1)

    meta_go = exchange(0, lambda to: meta_hbm.at[to], meta_in.at[me])
    key_go = exchange(2, lambda to: key_hbm.at[to], pair_in.at[me, :, width:])
    query_go = exchange(1, lambda to: query_hbm.at[to], pair_in.at[me, :, :width])

    tri_rows = tokens // 8

    @pl.loop(0, 8)
    def _(step):
        base = pl.multiple_of(step * tri_rows, tri_rows)
        before = lax.broadcasted_iota(jnp.int32, (tri_rows, tokens), 0) + base
        after = lax.broadcasted_iota(jnp.int32, (tri_rows, tokens), 1)
        score_low[pl.ds(base, tri_rows), :] = jnp.where(before < after, 1.0, 0.0).astype(
            jnp.bfloat16
        )

    arrive(meta_go)
    line = lax.broadcasted_iota(jnp.int32, (8, tokens), 0)
    line_float = line.astype(jnp.float32)
    base_count = jnp.zeros((8, 1), jnp.float32)
    lines = jnp.zeros((8, tokens), jnp.float32)
    for b in range(sources):
        first, last = spans[b]
        cluster = meta_in[b, 0:1, :]
        hits = jnp.where(cluster == line_float, 1.0, 0.0)
        rank = jnp.dot(
            hits.astype(jnp.bfloat16), score_low[...], preferred_element_type=jnp.float32
        )
        target = jnp.sum(hits * (rank + base_count), axis=0, keepdims=True)
        base_count = base_count + jnp.sum(hits, axis=1, keepdims=True)
        slot = cluster * float(last - first) + target - float(first)
        lines = jnp.where(line == b, slot, lines)
    key_lines[...] = lines
    key_cols[...] = jnp.transpose(lines)

    for b in range(sources):
        first, last = spans[b]
        many = clusters * (last - first)

        @pl.loop(0, many // 64)
        def _(step, b=b):
            base = pl.multiple_of(step * 64, 64)
            at = (lax.broadcasted_iota(jnp.int32, (64, tokens), 0) + base).astype(jnp.float32)
            pick[b][pl.ds(base, 64), :] = jnp.where(
                at == key_lines[b : b + 1, :], 1.0, 0.0
            ).astype(jnp.bfloat16)

        @pl.loop(0, tokens // 64)
        def _(step, b=b, many=many):
            base = pl.multiple_of(step * 64, 64)
            at = lax.broadcasted_iota(jnp.int32, (64, many), 1).astype(jnp.float32)
            unpick[b][pl.ds(base, 64), :] = jnp.where(
                at == key_cols[pl.ds(base, 64), b : b + 1], 1.0, 0.0
            ).astype(jnp.bfloat16)

    def gather(block_at, out, lanes=slice(None), together=2):
        for b in range(sources):
            first, last = spans[b]
            size = last - first
            shared = spans[b - 1][1] - first if b > 0 else 0
            block = block_at(b)


            @pl.loop(0, clusters // together)
            def _(step, b=b, first=first, last=last, size=size, shared=shared, block=block):
                base = pl.multiple_of(step * together * size, 64)
                found = jnp.dot(
                    pick[b][pl.ds(base, together * size), :],
                    block,
                    preferred_element_type=jnp.float32,
                )
                for at in range(together):
                    c = step * together + at
                    part = found[at * size : (at + 1) * size]
                    if shared > 0:
                        out[c, first : first + shared, lanes] = (
                            out[c, first : first + shared, lanes].astype(jnp.float32)
                            + part[:shared]
                        ).astype(out.dtype)
                    out[c, first + shared : last, lanes] = part[shared:].astype(out.dtype)

    gather(lambda b: jnp.transpose(meta_in[b]).astype(jnp.bfloat16), place_col)

    @pl.loop(0, clusters)
    def _(c):
        place_row[c] = jnp.transpose(place_col[c])

    arrive(key_go)
    grad_go = exchange(3, lambda to: grad_hbm.at[to], grad_in.at[me])
    gather(lambda b: pair_in[b, :, width:], pair_rows, slice(width, 2 * width))

    @pl.loop(0, clusters)
    def _(c):
        keys = pair_rows[c, :, width:].astype(jnp.float32)
        unit = keys * lax.rsqrt(jnp.sum(keys * keys, axis=1, keepdims=True) + epsilon)
        centroid_out[c] = jnp.broadcast_to(jnp.sum(unit, axis=0, keepdims=True), (8, width))

    centroid_go = exchange(5, lambda to: centroid_out.at[to], centroid_hbm.at[me])

    arrive(query_go)
    value_go = exchange(4, lambda to: value_hbm.at[to], value_in.at[me])
    gather(lambda b: pair_in[b, :, :width], pair_rows, slice(0, width))

    tile = min(256, rows)
    tiles = rows // tile

    @pl.loop(0, clusters * tiles)
    def _(step):
        c = step // tiles
        base = pl.multiple_of((step % tiles) * tile, tile)
        scores = lax.dot_general(
            pair_rows[c, :, width:],
            pair_rows[c, pl.ds(base, tile), :width],
            (((1,), (1,)), ((), ())),
            preferred_element_type=jnp.float32,
        )
        place_u = place_col[c, :, 1:2] * 64.0 + place_col[c, :, 2:3]
        place_t = (
            place_row[c, 1:2, pl.ds(base, tile)] * 64.0 + place_row[c, 2:3, pl.ds(base, tile)]
        )
        scores = jnp.where(place_u <= place_t, scores, -1e30)
        highest = jnp.max(scores, axis=0, keepdims=True)
        terms = jnp.exp2((scores - highest) * (scale * 1.4426950408889634))
        inverse = 1.0 / jnp.sum(terms, axis=0, keepdims=True)
        weights[c, :, pl.ds(base, tile)] = terms * inverse

    def go_home(source, home, lanes, array, target):
        half = sources // 2
        turn = tokens

        @pl.loop(0, sources)
        def _(step):
            late = step // half
            d = (half + step) * (1 - late) + (sources - 1 - step) * late
            to = peer(d)
            for b in range(sources):

                @pl.when(to == b)
                def _(b=b):
                    first, last = spans[b]
                    size = last - first
                    for c in range(clusters):
                        stacked[c * size : (c + 1) * size, :] = source[c, first:last, :]

                    @pl.loop(0, tokens // turn)
                    def _(part):
                        base = pl.multiple_of(part * turn, turn)
                        home[b, pl.ds(base, turn), lanes] = jnp.dot(
                            unpick[b][pl.ds(base, turn), :],
                            stacked[: clusters * size, :],
                            preferred_element_type=jnp.float32,
                        ).astype(jnp.bfloat16)

            @pl.when(step < sources - 1)
            def _():
                remote(array, d, home.at[to, :, lanes], target.at[me]).start()

        own = pltpu.make_async_copy(home.at[me, :, lanes], target.at[me], local_sem.at[array])
        own.start()
        return [
            remote(array, d, home.at[peer(d), :, lanes], target.at[me])
            for d in range(1, sources)
        ] + [own]

    arrive(grad_go)
    gather(lambda b: grad_in[b], grad_rows, together=clusters)

    @pl.loop(0, clusters)
    def _(c):
        dvalue_rows[c] = jnp.dot(
            weights[c].astype(jnp.bfloat16), grad_rows[c], preferred_element_type=jnp.float32
        ).astype(jnp.bfloat16)

    home_go = go_home(dvalue_rows, grad_in, slice(None), 6, dvalue_hbm)

    arrive(value_go)
    gather(lambda b: value_in[b], value_rows, together=clusters)

    @pl.loop(0, clusters)
    def _(c):
        keys_turned = jnp.transpose(pair_rows[c, :, width:])

        @pl.loop(0, tiles)
        def _(step):
            base = pl.multiple_of(step * tile, tile)
            prob = lax.dot_general(
                value_rows[c],
                grad_rows[c, pl.ds(base, tile), :],
                (((1,), (1,)), ((), ())),
                preferred_element_type=jnp.float32,
            )
            part = weights[c, :, pl.ds(base, tile)]
            part_low = part.astype(jnp.bfloat16).astype(jnp.float32)
            delta = jnp.sum(part_low * prob, axis=0, keepdims=True)
            score_grad = (part * (prob - delta)).astype(jnp.bfloat16)
            score_low[:, pl.ds(base, tile)] = score_grad
            turned = jnp.dot(keys_turned, score_grad, preferred_element_type=jnp.float32)
            dquery_rows[c, pl.ds(base, tile), :] = jnp.transpose(turned * scale).astype(
                jnp.bfloat16
            )

        dkey_rows[c] = (
            jnp.dot(
                score_low[...], pair_rows[c, :, :width], preferred_element_type=jnp.float32
            )
            * scale
        ).astype(jnp.bfloat16)

    home_go += go_home(dquery_rows, pair_in, slice(0, width), 7, dquery_hbm)
    home_go += go_home(dkey_rows, pair_in, slice(width, 2 * width), 8, dkey_hbm)

    arrive(centroid_go)
    for copies, _own in (meta_go, query_go, key_go, grad_go, value_go, centroid_go):
        for copy in copies:
            copy.wait_send()
    for copy in home_go:
        copy.wait()


def per_device_heads(query_rows, key_rows, value_rows, grad_rows, clusters, positions):
    tokens, heads, width = query_rows.shape
    sources = lax.axis_size("seq")
    total = tokens
    share = tokens // sources
    spans = [
        span_of(b, sources, total, share - share // 4, share + share // 4) for b in range(sources)
    ]
    places = jnp.broadcast_to(positions[None, :], (heads, tokens))
    blank = jnp.zeros_like(places)
    meta = jnp.stack(
        [clusters, places // 64, places % 64, blank, blank, blank, blank, blank], axis=1
    ).astype(jnp.float32)
    by_head = [
        jnp.transpose(rows, (1, 0, 2)) for rows in (query_rows, key_rows, grad_rows, value_rows)
    ]
    anywhere = pl.BlockSpec(memory_space=pl.ANY)
    rows_shape = jax.ShapeDtypeStruct((heads, tokens, width), jnp.bfloat16)
    low = jnp.bfloat16
    full = jnp.float32
    sizes = [sources * (last - first) for first, last in spans]
    scratch = [
        pltpu.VMEM((sources, 8, tokens), full),
        pltpu.VMEM((sources, tokens, 2 * width), low),
        pltpu.VMEM((sources, tokens, width), low),
        pltpu.VMEM((sources, tokens, width), low),
        pltpu.VMEM((sources, total, 2 * width), low),
        pltpu.VMEM((sources, total, width), low),
        pltpu.VMEM((sources, total, width), low),
        pltpu.VMEM((sources, total, 8), full),
        pltpu.VMEM((sources, 8, total), full),
        pltpu.VMEM((8, tokens), full),
        pltpu.VMEM((tokens, 8), full),
        pltpu.VMEM((sources, total, total), full),
        pltpu.VMEM((total, total), low),
        pltpu.VMEM((sources, total, width), low),
        pltpu.VMEM((sources, total, width), low),
        pltpu.VMEM((sources, total, width), low),
        pltpu.VMEM((max(sizes), width), low),
        pltpu.VMEM((sources, 8, width), full),
        pltpu.SemaphoreType.DMA((9, sources - 1)),
        pltpu.SemaphoreType.DMA((9, sources - 1)),
        pltpu.SemaphoreType.DMA((9,)),
    ]
    scratch += [pltpu.VMEM((size, tokens), low) for size in sizes]
    scratch += [pltpu.VMEM((tokens, size), low) for size in sizes]
    outs = pl.pallas_call(
        functools.partial(exchange_kernel, sources, spans),
        out_shape=(
            rows_shape,
            rows_shape,
            rows_shape,
            jax.ShapeDtypeStruct((heads, 8, width), full),
        ),
        in_specs=[anywhere] * 5,
        out_specs=(anywhere,) * 4,
        scratch_shapes=scratch,
        compiler_params=pltpu.CompilerParams(
            collective_id=0, has_side_effects=True, vmem_limit_bytes=62 * 1024 * 1024
        ),
    )(meta, *by_head)
    dquery, dkey, dvalue = [jnp.transpose(rows, (1, 0, 2)) for rows in outs[:3]]
    return dquery, dkey, dvalue, outs[3][:, 0:1, :]


def solution(mesh):
    sources = mesh.shape["seq"]

    def body(query_rows, *others):
        if query_rows.shape[1] == sources and sources % 2 == 0 and CL_DEV == 1:
            return per_device_heads(query_rows, *others)
        return per_device(query_rows, *others)

    return jax.shard_map(
        body,
        mesh=mesh,
        in_specs=(
            P(("groups", "seq"), "head", None),
            P(("groups", "seq"), "head", None),
            P(("groups", "seq"), "head", None),
            P(("groups", "seq"), "head", None),
            P("head", ("groups", "seq")),
            P(("groups", "seq")),
        ),
        out_specs=(
            P(("groups", "seq"), "head", None),
            P(("groups", "seq"), "head", None),
            P(("groups", "seq"), "head", None),
            P("head", ("groups", "seq"), None),
        ),
        check_vma=False,
    )
```
